512 devices in a mesh: replica: 16 (over z_lo, y), section: 4 (over z_hi), tp: 8 (over x, core).
Axes of the slice: x: 4, y: 4, z: 16 (z_hi: 4, z_lo: 4; z = z_hi * 4 + z_lo), core: 2. Of those that a mesh axis runs over, the one named last changes fastest.
Arguments:
- hidden_in: bfloat16 [2048, 8192], P('replica', 'tp'), may hold values from -6 to 6
- gains: float32 [4, 8192], P('section', 'tp'), may hold values from 0.5 to 2
- weights: bfloat16 [4, 8192, 16, 512], P('section', 'tp', 'replica'), may hold values from -0.0625 to 0.0625
- lengths: int32 [16], P('replica'), may hold values from 1 to 128, 1536 in all
Outputs:
- states: bfloat16 [4, 2048, 8192], P('section', 'replica', 'tp')
The draws below stay inside these ranges and needn't reach their ends.
Inputs may be any that keep to these rules, and one draw needn't show every extreme that they name: One replica's prompt fills all 128 slots; the lengths sum to 3 * 2048 // 4 (integer division).
All inputs are finite; a program needn't handle non-finite values. No bound on the sum of `lengths` on one device may be relied on, other than what follows from the above.
Results may differ from the reference program's by a relative error of at most 0.025.
Values may be sent and summed in bfloat16 or wider, within the bound.
A program may use at most 64 MiB of HBM per device.

```python
import math
import jax
import jax.numpy as jnp
import numpy as np
from jax import lax

D = 8192
TOK_REP = 128
LAYERS = 4
TOKENS = 2048
COLW = 64
N_REPLICA = 16
N_TP = 8


def levels(rng, dims, shards, low, high):
    level, own = 1.0, jax.random.fold_in(rng, 6)
    for position, blocks in shards:
        steps = jnp.exp(jax.random.uniform(jax.random.fold_in(own, position), (blocks,), jnp.float32, low / len(shards), high / len(shards)))
        level = level * jnp.repeat(steps, dims[position] // blocks).reshape([-1 if axis == position else 1 for axis in range(len(dims))])
    return level


def profile(amount, total, reach, slope):
    weights = [(1 << 20) // math.isqrt(rank ** slope) + 1 for rank in range(2, amount + 1)]
    rest, given = total - reach - (amount - 1), [1] * (amount - 1)
    while rest > 0:
        free = [i for i in range(amount - 1) if given[i] < reach]
        pool, budget = sum([weights[i] for i in free]), rest
        for i in free:
            addition = min(reach - given[i], max(1, budget * weights[i] // pool), rest)
            given[i] = given[i] + addition
            rest = rest - addition
    return np.array([reach] + given)


def ragged(rng, count, total, most, slope):
    if count == 2:
        one = jax.random.randint(rng, (), max(1, total - most), min(most, total - 1) + 1)
        return jnp.stack([one, total - one])
    tallies = jnp.asarray(profile(count, total, most, slope), jnp.int32)
    couples = (count - 1) // 2
    giver, sink = tallies[1:1 + 2 * couples:2], tallies[2:2 + 2 * couples:2]
    margin = jnp.minimum(giver - 1, most - sink)
    shifted = jax.random.randint(jax.random.fold_in(rng, 1), (couples,), 0, 1 << 20) % (margin + 1)
    tallies = tallies.at[1:1 + 2 * couples:2].set(giver - shifted).at[2:2 + 2 * couples:2].set(sink + shifted)
    return tallies[jax.random.permutation(jax.random.fold_in(rng, 2), count)]


def scatter_about(rng, dims, spread, most, split=(), kind=jnp.bfloat16):
    array = spread * jax.random.normal(rng, dims, jnp.float32)
    if split:
        array = array * levels(rng, dims, split, -0.22, 0.18)
    return jnp.clip(array, -most, most).astype(kind)


def setup_inputs(seed: int = 0) -> dict:
    key_list = jax.random.split(jax.random.key(seed), 5)
    hidden_in = scatter_about(key_list[0], (TOKENS, D), 1.0, 6.0, ((0, 16), (1, 8)))
    gains = jnp.clip(jnp.exp(math.log(2.0) - 1.3862944 * jax.random.uniform(key_list[1], (LAYERS, D), jnp.float32) ** levels(key_list[1], (LAYERS, D), ((0, 4), (1, 8)), -0.2, 0.2)), 0.5, 2.0)
    weights = scatter_about(key_list[2], (LAYERS, D, N_REPLICA, N_TP * COLW), D ** -0.5, 0.0625, ((0, 4), (1, 8), (2, 16)))
    lengths = ragged(key_list[3], N_REPLICA, N_REPLICA * TOK_REP * 3 // 4, TOK_REP, 1).astype(jnp.int32)
    return dict(hidden_in=hidden_in, gains=gains, weights=weights, lengths=lengths)


EPSILON = 1e-06

def reference(hidden_in, gains, weights, lengths):
    tokens_all = hidden_in.shape[0]
    model_width = hidden_in.shape[1]
    feat_block = model_width // N_TP
    col_width = model_width // (N_TP * N_REPLICA)
    weights_flat = weights.reshape(LAYERS, model_width, N_REPLICA, N_TP, col_width)
    weights_flat = jnp.transpose(weights_flat, (0, 1, 3, 2, 4)).reshape(LAYERS, model_width, model_width)
    row_ids = jnp.arange(tokens_all, dtype=jnp.int32)
    prompt = row_ids // TOK_REP
    is_valid = row_ids % TOK_REP < lengths[prompt]
    hidden = hidden_in
    outputs = []
    for layer_id in range(LAYERS):
        widened = hidden.astype(jnp.float32)
        squares_sum = lax.optimization_barrier(jnp.sum(widened * widened, axis=1, keepdims=True))
        inverse = lax.rsqrt(squares_sum / model_width + EPSILON)
        scaled = (widened * gains[layer_id][None, :]).astype(jnp.bfloat16)
        accum = jnp.zeros((tokens_all, model_width), jnp.float32)
        for shard_id in range(N_TP):
            lower = shard_id * feat_block
            term_part = jnp.dot(scaled[:, lower:lower + feat_block], weights_flat[layer_id, lower:lower + feat_block, :], preferred_element_type=jnp.float32)
            rounded = lax.optimization_barrier(term_part.astype(jnp.bfloat16))
            accum = accum + rounded.astype(jnp.float32)
        hidden = (widened + inverse * accum).astype(jnp.bfloat16)
        outputs.append(jnp.where(is_valid[:, None], hidden, jnp.zeros_like(hidden)))
    return jnp.stack(outputs)
```

```python
import functools

import jax
import jax.numpy as jnp
from jax import lax
from jax.experimental import pallas as pl
from jax.experimental.pallas import tpu as pltpu
from jax.sharding import PartitionSpec as P

EPSILON = 1e-06
MESH = pl.DeviceIdType.MESH
NEAR_Y = 4
CORES = 2
ROWS = 16
LANES = 128

STAGES = dict(scale=0.0, along_y=3.0, onward=6.5, product=9.0, pair=10.5, along_x=14.0, update=17.0)
INTERVAL = 5.0


def order_of(slabs):
    events = [
        (slab * INTERVAL + offset, slab, name)
        for slab in range(slabs)
        for name, offset in STAGES.items()
    ]
    return [(name, slab) for _, slab, name in sorted(events, key=lambda e: (e[0], e[1]))]


def kernel(
    sizes, hid_ref, gain_ref, w_ref, out_ref,
    held, gathered, squares, own, core_out, core_in, x_out, x_in, page_out, page_in, inverse,
    hop_s, hop_r, z_s, z_r, y_s, y_r, f_s, f_r, c_s, c_r, x_s, x_r, p_s, p_r,
):
    replicas, sections, groups, slabs = sizes
    near_y, near_z, near_x = NEAR_Y, replicas // NEAR_Y, groups // CORES
    half_y, half_z = near_y // 2, near_z // 2
    share = half_y * near_z
    width = hid_ref.shape[1]
    page = w_ref.shape[1]
    half_rows = share * ROWS

    replica, section, tp = lax.axis_index("replica"), lax.axis_index("section"), lax.axis_index("tp")
    z, y = replica // near_y, replica % near_y
    x, core = tp // CORES, tp % CORES
    other = 1 - core
    up_y, down_y = (y + 1) % near_y, (y + near_y - 1) % near_y

    def place(z_to=z, y_to=y, x_to=x, core_to=core, section_to=section):
        return (z_to * near_y + y_to, section_to, x_to * CORES + core_to)

    def send(src, dst, send_sem, recv_sem, device):
        pltpu.make_async_remote_copy(
            src_ref=src, dst_ref=dst, send_sem=send_sem, recv_sem=recv_sem, device_id=device, device_id_type=MESH
        ).start()

    def wait(ref, sem):
        pltpu.make_async_copy(ref, ref, sem).wait()

    lane = lax.broadcasted_iota(jnp.int32, (ROWS, LANES), 1)
    low = lane < LANES // 2

    def two_parts(value):
        high = value.astype(jnp.bfloat16).astype(jnp.float32)
        return jnp.where(low, high, value - high)

    def one_value(parts):
        return parts + pltpu.roll(parts, LANES // 2, 1)

    barrier = pltpu.get_barrier_semaphore()

    def greet(device):
        pl.semaphore_signal(barrier, inc=1, device_id=device, device_id_type=MESH)

    greeted = 0
    for dz in range(near_z):
        for dy in range(near_y):
            for dc in range(CORES):
                if dz or dy or dc:
                    greet(place((z + dz) % near_z, (y + dy) % near_y, core_to=(core + dc) % CORES))
                    greeted += 1
    for dx in range(1, near_x):
        greet(place(x_to=(x + dx) % near_x))
        greeted += 1

    @pl.when(section > 0)
    def _():
        greet(place(section_to=section - 1))

    @pl.when(section == 0)
    def _():
        held[...] = hid_ref[...].reshape(held.shape)

    pl.semaphore_wait(barrier, greeted + jnp.where(section < sections - 1, 1, 0))

    def scale(m):
        @pl.when(section > 0)
        def _():
            wait(held.at[m], hop_r.at[m])

        rows = held[m].astype(jnp.float32)
        total = jnp.sum(rows * rows, axis=1, keepdims=True)
        squares[m] = two_parts(jnp.broadcast_to(total, (ROWS, LANES)))
        gathered[m, y, z] = (rows * gain_ref[...]).astype(jnp.bfloat16)
        for dz in range(1, near_z):
            block = gathered.at[m, y, z]
            send(block, block, z_s.at[m], z_r.at[m], place(z_to=(z + dz) % near_z))

    def along_y(m):
        wait(gathered.at[m, y, pl.ds(0, near_z - 1)], z_r.at[m])
        block = gathered.at[m, y]
        send(block, block, y_s.at[m, 0], y_r.at[m, 0], place(y_to=up_y))
        send(block, block, y_s.at[m, 1], y_r.at[m, 1], place(y_to=down_y))

    def onward(m):
        wait(gathered.at[m, down_y], y_r.at[m, 0])
        block = gathered.at[m, down_y, pl.ds(0, half_z)]
        send(block, block, f_s.at[m, 0], f_r.at[m, 0], place(y_to=up_y))
        wait(gathered.at[m, up_y], y_r.at[m, 1])
        block = gathered.at[m, up_y, pl.ds(half_z, half_z)]
        send(block, block, f_s.at[m, 1], f_r.at[m, 1], place(y_to=down_y))

    def product(m):
        opposite = (y + 2) % near_y
        wait(gathered.at[m, opposite, pl.ds(0, half_z)], f_r.at[m, 0])
        wait(gathered.at[m, opposite, pl.ds(half_z, half_z)], f_r.at[m, 1])

        def times(core_of):
            rows = gathered[m, pl.ds(core_of * half_y, half_y)].reshape(half_rows, width)
            return jnp.dot(rows, w_ref[...], preferred_element_type=jnp.float32)

        core_out[m, pl.ds(0, half_rows)] = times(other).astype(jnp.bfloat16)
        core_out[m, pl.ds(half_rows, ROWS)] = jnp.concatenate(
            [squares[m].astype(jnp.bfloat16)] * (page // LANES), axis=1
        )
        send(core_out.at[m], core_in.at[m], c_s.at[m], c_r.at[m], place(core_to=other))
        own[m] = times(core)

    def pair(m):
        wait(core_in.at[m], c_r.at[m])
        total = (own[m] + core_in[m, pl.ds(0, half_rows)].astype(jnp.float32)).astype(jnp.bfloat16)
        parts = squares[m] + core_in[m, pl.ds(half_rows, ROWS), pl.ds(0, LANES)].astype(jnp.float32)
        parts = two_parts(one_value(parts)).astype(jnp.bfloat16)
        for j in range(near_x):
            x_out[m, j, pl.ds(0, half_rows)] = total[:, j * LANES : (j + 1) * LANES]
            x_out[m, j, pl.ds(half_rows, ROWS)] = parts
        for dx in range(1, near_x):
            to = (x + dx) % near_x
            send(x_out.at[m, to], x_in.at[m, dx - 1], x_s.at[m], x_r.at[m], place(x_to=to))

    def along_x(m):
        wait(x_in.at[m], x_r.at[m])
        total = x_out[m, x].astype(jnp.float32)
        for dx in range(1, near_x):
            total += x_in[m, dx - 1].astype(jnp.float32)
        page_out[m] = total[:half_rows].astype(jnp.bfloat16).reshape(share, ROWS, LANES)
        mean = one_value(total[half_rows:]) / (width * groups)
        inverse[m] = lax.rsqrt(mean + EPSILON)
        for j in range(share):
            z_to, y_to = j % near_z, core * half_y + j // near_z
            src, dst = page_out.at[m, j], page_in.at[m, replica]
            here = (z_to == z) & (y_to == y)

            @pl.when(here)
            def _(src=src, dst=dst):
                pltpu.make_async_copy(src, dst, p_r.at[m]).start()

            @pl.when(jnp.logical_not(here))
            def _(src=src, dst=dst, z_to=z_to, y_to=y_to):
                send(src, dst, p_s.at[m], p_r.at[m], place(z_to, y_to))

            send(src, dst, p_s.at[m], p_r.at[m], place(z_to, y_to, core_to=other))

    def update(m):
        wait(page_in.at[m], p_r.at[m])
        first = core == 0
        for k in range(replicas // 2):
            even = page_in[m, 2 * k].astype(jnp.float32)
            odd = page_in[m, 2 * k + 1].astype(jnp.float32)
            turned = pltpu.roll(jnp.where(first, odd, even), LANES // 2, 1)
            block = jnp.where(low, jnp.where(first, even, turned), jnp.where(first, turned, odd))
            columns = pl.ds(k * LANES, LANES)
            new = held[m, :, columns].astype(jnp.float32) + inverse[m] * block
            out_ref[pl.ds(m * ROWS, ROWS), columns] = new.astype(jnp.bfloat16)

        @pl.when(section < sections - 1)
        def _():
            send(
                out_ref.at[pl.ds(m * ROWS, ROWS)], held.at[m], hop_s.at[m], hop_r.at[m],
                place(section_to=section + 1),
            )

    stages = dict(scale=scale, along_y=along_y, onward=onward, product=product, pair=pair, along_x=along_x, update=update)
    for name, m in order_of(slabs):
        with jax.named_scope(name):
            stages[name](m)

    among = y // half_y == core
    for m in range(slabs):
        wait(gathered.at[m, 0, pl.ds(0, near_z - 1)], z_s.at[m])
        for way in range(2):
            wait(gathered.at[m, 0], y_s.at[m, way])
            wait(gathered.at[m, 0, pl.ds(0, half_z)], f_s.at[m, way])
        wait(core_out.at[m], c_s.at[m])
        wait(x_in.at[m], x_s.at[m])

        @pl.when(among)
        def _(m=m):
            wait(page_in.at[m, pl.ds(0, CORES * share - 1)], p_s.at[m])

        @pl.when(jnp.logical_not(among))
        def _(m=m):
            wait(page_in.at[m], p_s.at[m])

        @pl.when(section < sections - 1)
        def _(m=m):
            wait(held.at[m], hop_s.at[m])


def local(sizes, hidden_in, gains, weights, lengths):
    replicas, sections, groups = sizes
    slots, width = hidden_in.shape
    page = weights.shape[3]
    slabs = slots // ROWS
    near_z, near_x = replicas // NEAR_Y, groups // CORES
    share = replicas // CORES
    block = share * ROWS + ROWS
    bf16, f32 = jnp.bfloat16, jnp.float32
    dma = pltpu.SemaphoreType.DMA
    states = pl.pallas_call(
        functools.partial(kernel, (*sizes, slabs)),
        out_shape=jax.ShapeDtypeStruct((slots, width), bf16),
        in_specs=[pl.BlockSpec(memory_space=pltpu.VMEM)] * 3,
        out_specs=pl.BlockSpec(memory_space=pltpu.VMEM),
        scratch_shapes=[
            pltpu.VMEM((slabs, ROWS, width), bf16),
            pltpu.VMEM((slabs, NEAR_Y, near_z, ROWS, width), bf16),
            pltpu.VMEM((slabs, ROWS, LANES), f32),
            pltpu.VMEM((slabs, share * ROWS, page), f32),
            pltpu.VMEM((slabs, block, page), bf16),
            pltpu.VMEM((slabs, block, page), bf16),
            pltpu.VMEM((slabs, near_x, block, LANES), bf16),
            pltpu.VMEM((slabs, near_x - 1, block, LANES), bf16),
            pltpu.VMEM((slabs, share, ROWS, LANES), bf16),
            pltpu.VMEM((slabs, replicas, ROWS, LANES), bf16),
            pltpu.VMEM((slabs, ROWS, LANES), f32),
            dma((slabs,)), dma((slabs,)),
            dma((slabs,)), dma((slabs,)),
            dma((slabs, 2)), dma((slabs, 2)),
            dma((slabs, 2)), dma((slabs, 2)),
            dma((slabs,)), dma((slabs,)),
            dma((slabs,)), dma((slabs,)),
            dma((slabs,)), dma((slabs,)),
        ],
        compiler_params=pltpu.CompilerParams(
            collective_id=0, has_side_effects=True, vmem_limit_bytes=40 << 20
        ),
        name="layer_sections",
    )(hidden_in, gains, weights.reshape(width, page))
    positions = jnp.arange(slots, dtype=jnp.int32)
    return jnp.where((positions < lengths[0])[:, None], states, jnp.zeros_like(states))[None]


def solution(mesh):
    sizes = tuple(mesh.shape[axis] for axis in ("replica", "section", "tp"))
    return jax.shard_map(
        functools.partial(local, sizes),
        mesh=mesh,
        in_specs=(
            P("replica", "tp"),
            P("section", "tp"),
            P("section", "tp", "replica", None),
            P("replica"),
        ),
        out_specs=P("section", "replica", "tp"),
        check_vma=False,
    )
```

```python
import functools

import jax
import jax.numpy as jnp
from jax import lax
from jax.experimental import pallas as pl
from jax.experimental.pallas import tpu as pltpu
from jax.sharding import PartitionSpec as P

EPSILON = 1e-06
MESH = pl.DeviceIdType.MESH
NEAR_Y = 4
CORES = 2
ROWS = 8
HIGH = 16
LANES = 128
HALF = LANES // 2
BATCH = 2 * HIGH // ROWS

STAGES = dict(along_z=0.0, along_y=4, product=9, pair=10.5, update=14)
PAGES, PLACE = 14.1, 60
INTERVAL = 3


def order_of(slabs):
    events = [(m * INTERVAL + offset, m, name) for m in range(slabs) for name, offset in STAGES.items()]
    for batch in range(slabs // BATCH):
        last = (batch + 1) * BATCH - 1
        events += [(last * INTERVAL + PAGES, batch, "pages"), (last * INTERVAL + PLACE, batch, "place")]
    return [(name, index) for _, index, name in sorted(events, key=lambda e: (e[0], e[1]))]


def kernel(
    sizes, hid_hbm, gain_hbm, w_hbm, out_ref,
    hid_ref, gain_ref, w_ref,
    gathered, scaled, prod, residual, squares, mine, core_out, core_in, x_out, x_in, new_out, page_out, page_in,
    in_sem, hop_s, hop_r, z_s, z_r, e_s, e_r, y_s, y_r, c_s, c_r, x_s, x_r, p_s, p_r,
):
    replicas, sections, groups, slabs = sizes
    near_y, near_z, near_x = NEAR_Y, replicas // NEAR_Y, groups // CORES
    row_groups = replicas * ROWS // HIGH
    tiles = row_groups // 2
    width = hid_ref.shape[1]
    column_tiles = width // LANES
    bf16, f32 = jnp.bfloat16, jnp.float32

    replica, section, tp = lax.axis_index("replica"), lax.axis_index("section"), lax.axis_index("tp")
    z, y = replica // near_y, replica % near_y
    x, core = tp // CORES, tp % CORES

    def place_of(z_to=z, y_to=y, x_to=x, core_to=core, section_to=section):
        return (z_to * near_y + y_to, section_to, x_to * CORES + core_to)

    def send(src, dst, send_sem, recv_sem, device):
        pltpu.make_async_remote_copy(
            src_ref=src, dst_ref=dst, send_sem=send_sem, recv_sem=recv_sem, device_id=device, device_id_type=MESH
        ).start()

    def wait(ref, sem):
        pltpu.make_async_copy(ref, ref, sem).wait()

    lane = lax.broadcasted_iota(jnp.int32, (HIGH, LANES), 1)
    low = lane < HALF
    high_part = lane % 8 < 4

    def turn(value):
        return pltpu.roll(value, HALF, 1)

    def lows(left, right):
        return jnp.where(low, left, turn(right))

    def highs(left, right):
        return jnp.where(low, turn(left), right)

    def two_parts(value):
        high = value.astype(bf16).astype(f32)
        return jnp.where(high_part, high, value - high)

    def one_value(parts):
        return parts + jnp.where(high_part, pltpu.roll(parts, LANES - 4, 1), pltpu.roll(parts, 4, 1))

    def stack(above, below):
        return jnp.concatenate([above, below], axis=0)

    def slot_of(z_from):
        return (z_from - z + near_z) % near_z

    def load_hidden():
        return pltpu.make_async_copy(hid_hbm, hid_ref, in_sem.at[0])

    def load_gains():
        return pltpu.make_async_copy(gain_hbm, gain_ref, in_sem.at[1])

    def load_weights():
        return pltpu.make_async_copy(w_hbm, w_ref, in_sem.at[2])

    @pl.when(section == 0)
    def _():
        load_hidden().start()

    load_gains().start()
    load_weights().start()

    barrier = pltpu.get_barrier_semaphore()

    def greet(device):
        pl.semaphore_signal(barrier, inc=1, device_id=device, device_id_type=MESH)

    @pl.when(section > 0)
    def _():
        greet(place_of(section_to=section - 1))

    for dz in range(near_z):
        for dy in range(near_y):
            if dz or dy:
                greet(place_of((z + dz) % near_z, (y + dy) % near_y))
    greet(place_of(core_to=1 - core))
    for dx in range(1, near_x):
        greet(place_of(x_to=(x + dx) % near_x))

    @pl.when(section == 0)
    def _():
        load_hidden().wait()

        def of_pair(pair, _):
            rows = pl.ds(pl.multiple_of(pair * HIGH, HIGH), HIGH)
            for t in range(tiles):
                left = hid_ref[rows, pl.ds(t * LANES, LANES)].astype(f32)
                right = hid_ref[rows, pl.ds((t + tiles) * LANES, LANES)].astype(f32)
                gathered[2 * pair, y, 0, t] = stack(left[:ROWS], right[:ROWS]).astype(bf16)
                gathered[2 * pair + 1, y, 0, t] = stack(left[ROWS:], right[ROWS:]).astype(bf16)
            return 0

        lax.fori_loop(0, slabs // 2, of_pair, 0)

    pl.semaphore_wait(barrier, replicas + near_x - 1 + jnp.where(section < sections - 1, 1, 0))

    def along_z(m):
        block = gathered.at[m, y, 0]

        @pl.when(section > 0)
        def _():
            wait(block, hop_r.at[m])

        for dz in range(1, near_z):
            send(block, gathered.at[m, y, near_z - dz], z_s.at[m], z_r.at[m], place_of(z_to=(z + dz) % near_z))
        for dy in range(1, near_y):
            send(block, block, e_s.at[m], e_r.at[m], place_of(y_to=(y + dy) % near_y))

    def along_y(m):
        block = gathered.at[m, y, pl.ds(1, near_z - 1)]
        wait(block, z_r.at[m])
        for dy in range(1, near_y):
            send(block, block, y_s.at[m], y_r.at[m], place_of(y_to=(y + dy) % near_y))

    def product(m):
        wait(gathered.at[m, pl.ds(0, near_y - 1), 0], e_r.at[m])
        wait(gathered.at[m, pl.ds(0, near_y - 1), pl.ds(1, near_z - 1)], y_r.at[m])

        def add_square(total, group, value):
            return total + jnp.where(lane // 8 == group, jnp.sum(value, axis=1, keepdims=True), 0.0)

        @pl.when(section == 0)
        def _():
            def chunks(group):
                y_from, z_from = 2 * group // near_z, 2 * group % near_z
                return y_from, slot_of(z_from), slot_of(z_from + 1)

            def of_group(group, total):
                y_from, first, second = chunks(group)
                acc = jnp.zeros((HIGH, LANES), f32)
                rows = pl.ds(pl.multiple_of(group * HIGH, HIGH), HIGH)
                for t in range(tiles):
                    one = gathered[m, y_from, first, t].astype(f32)
                    two = gathered[m, y_from, second, t].astype(f32)
                    for k, value in ((t, stack(one[:ROWS], two[:ROWS])), (t + tiles, stack(one[ROWS:], two[ROWS:]))):
                        columns = pl.ds(k * LANES, LANES)
                        acc += value * value
                        scaled[rows, columns] = (value * gain_ref[:, columns]).astype(bf16)
                return add_square(total, group, acc)

            squares[m] = two_parts(lax.fori_loop(0, row_groups, of_group, jnp.zeros((HIGH, LANES), f32)))
            odd = replica % 2 == 1
            column = replica // 2
            upper = column >= tiles

            def own_columns(group):
                y_from, first, second = chunks(group)
                one = gathered[m, y_from, first, column % tiles].astype(f32)
                two = gathered[m, y_from, second, column % tiles].astype(f32)
                return jnp.where(upper, stack(one[ROWS:], two[ROWS:]), stack(one[:ROWS], two[:ROWS]))

            for a in range(tiles):
                left, right = own_columns(a), own_columns(a + tiles)
                residual[m, a] = jnp.where(odd, highs(left, right), lows(left, right)).astype(bf16)

        @pl.when(section > 0)
        def _():
            def of_tile(a, total):
                acc = jnp.zeros((HIGH, LANES), f32)
                top = pl.ds(pl.multiple_of(a * HIGH, HIGH), HIGH)
                bottom = pl.ds(pl.multiple_of((a + tiles) * HIGH, HIGH), HIGH)
                for k in range(column_tiles):
                    columns = pl.ds(k * LANES, LANES)
                    gain = gain_ref[:, columns]
                    y_from, slot = 2 * k % near_y, slot_of(2 * k // near_y)
                    left = gathered[m, y_from, slot, a].astype(f32)
                    right = gathered[m, y_from + 1, slot, a].astype(f32)
                    acc += left * left + right * right
                    scaled[top, columns] = (lows(left, right) * gain).astype(bf16)
                    scaled[bottom, columns] = (highs(left, right) * gain).astype(bf16)
                total = add_square(total, a, jnp.where(low, acc, 0.0))
                return add_square(total, a + tiles, jnp.where(low, 0.0, acc))

            squares[m] = two_parts(lax.fori_loop(0, tiles, of_tile, jnp.zeros((HIGH, LANES), f32)))
            residual[m] = gathered[m, y, 0]

        prod[...] = jnp.dot(scaled[...], w_ref[...], preferred_element_type=f32)
        first_core = core == 0

        def split(a, _):
            top = pl.ds(pl.multiple_of(a * HIGH, HIGH), HIGH)
            bottom = pl.ds(pl.multiple_of((a + tiles) * HIGH, HIGH), HIGH)
            for j in range(near_x):
                columns = pl.ds(j * LANES, LANES)
                left, right = prod[top, columns], prod[bottom, columns]
                of_0, of_1 = lows(left, right), highs(left, right)
                mine[m, j, a] = jnp.where(first_core, of_0, of_1)
                core_out[m, j * tiles + a] = jnp.where(first_core, of_1, of_0).astype(bf16)
            return 0

        lax.fori_loop(0, tiles, split, 0)
        core_out[m, near_x * tiles] = squares[m].astype(bf16)
        send(core_out.at[m], core_in.at[m], c_s.at[m], c_r.at[m], place_of(core_to=1 - core))

    def pair(m):
        wait(core_in.at[m], c_r.at[m])
        parts = squares[m] + core_in[m, near_x * tiles].astype(f32)
        parts = two_parts(one_value(parts)).astype(bf16)
        for j in range(near_x):
            theirs = core_in[m, pl.ds(j * tiles, tiles)].astype(f32)
            x_out[m, j, pl.ds(0, tiles)] = (mine[m, j] + theirs).astype(bf16)
            x_out[m, j, tiles] = parts
        for dx in range(1, near_x):
            to = (x + dx) % near_x
            send(x_out.at[m, to], x_in.at[m, dx - 1], x_s.at[m], x_r.at[m], place_of(x_to=to))

    def update(m):
        wait(x_in.at[m], x_r.at[m])

        def total(a):
            value = x_out[m, x, a].astype(f32)
            for dx in range(1, near_x):
                value += x_in[m, dx - 1, a].astype(f32)
            return value

        inverse = lax.rsqrt(one_value(total(tiles)) / (width * groups) + EPSILON)
        for a in range(tiles):
            b = a + tiles
            factor = jnp.where(low, inverse[:, 8 * a : 8 * a + 1], inverse[:, 8 * b : 8 * b + 1])
            new_out[m, a] = (residual[m, a].astype(f32) + factor * total(a)).astype(bf16)

        @pl.when(section < sections - 1)
        def _():
            send(new_out.at[m], gathered.at[m, y, 0], hop_s.at[m], hop_r.at[m], place_of(section_to=section + 1))

    def pages(batch):
        for q in range(replicas):
            group, part = q * ROWS // HIGH, q * ROWS % HIGH
            piece = [
                new_out[batch * BATCH + i, group % tiles].astype(f32)[part : part + ROWS] for i in range(BATCH)
            ]
            left, right = stack(piece[0], piece[1]), stack(piece[2], piece[3])
            page_out[batch, q] = (lows if group < tiles else highs)(left, right).astype(bf16)
            y_to, z_to = q // near_z, q % near_z
            src, dst = page_out.at[batch, q], page_in.at[batch, replica]
            here = (z_to == z) & (y_to == y)

            @pl.when(here)
            def _(src=src, dst=dst):
                pltpu.make_async_copy(src, dst, p_r.at[batch]).start()

            @pl.when(jnp.logical_not(here))
            def _(src=src, dst=dst, z_to=z_to, y_to=y_to):
                send(src, dst, p_s.at[batch], p_r.at[batch], place_of(z_to, y_to))

    def place(batch):
        wait(page_in.at[batch], p_r.at[batch])
        row = batch * BATCH * ROWS
        for k in range(column_tiles):
            columns = pl.ds(k * LANES, LANES)
            left, right = page_in[batch, 2 * k].astype(f32), page_in[batch, 2 * k + 1].astype(f32)
            out_ref[pl.ds(row, HIGH), columns] = lows(left, right).astype(bf16)
            out_ref[pl.ds(row + HIGH, HIGH), columns] = highs(left, right).astype(bf16)

    stages = dict(
        along_z=along_z, along_y=along_y, product=product, pair=pair, update=update, pages=pages, place=place
    )
    loaded = False
    for name, index in order_of(slabs):
        if name == "product" and not loaded:
            load_gains().wait()
            load_weights().wait()
            loaded = True
        stages[name](index)

    for m in range(slabs):
        wait(gathered.at[m, 0, pl.ds(1, near_z - 1)], z_s.at[m])
        wait(gathered.at[m, pl.ds(0, near_y - 1), 0], e_s.at[m])
        wait(gathered.at[m, pl.ds(0, near_y - 1), pl.ds(1, near_z - 1)], y_s.at[m])
        wait(core_out.at[m], c_s.at[m])
        wait(x_in.at[m], x_s.at[m])

        @pl.when(section < sections - 1)
        def _(m=m):
            wait(new_out.at[m], hop_s.at[m])

    for batch in range(slabs // BATCH):
        wait(page_in.at[batch, pl.ds(0, replicas - 1)], p_s.at[batch])


def local(sizes, hidden_in, gains, weights, lengths):
    replicas, sections, groups = sizes
    slots, width = hidden_in.shape
    page = weights.shape[3]
    slabs = slots // ROWS
    batches = slabs // BATCH
    near_z, near_x = replicas // NEAR_Y, groups // CORES
    rows = replicas * ROWS
    tiles = rows // HIGH // 2
    bf16, f32 = jnp.bfloat16, jnp.float32
    tile = (HIGH, LANES)
    dma = pltpu.SemaphoreType.DMA
    states = pl.pallas_call(
        functools.partial(kernel, (*sizes, slabs)),
        out_shape=jax.ShapeDtypeStruct((slots, width), bf16),
        in_specs=[pl.BlockSpec(memory_space=pl.ANY)] * 3,
        out_specs=pl.BlockSpec(memory_space=pltpu.VMEM),
        scratch_shapes=[
            pltpu.VMEM((slots, width), bf16),
            pltpu.VMEM((1, width), f32),
            pltpu.VMEM((width, page), bf16),
            pltpu.VMEM((slabs, NEAR_Y, near_z, tiles, *tile), bf16),
            pltpu.VMEM((rows, width), bf16),
            pltpu.VMEM((rows, page), f32),
            pltpu.VMEM((slabs, tiles, *tile), bf16),
            pltpu.VMEM((slabs, *tile), f32),
            pltpu.VMEM((slabs, near_x, tiles, *tile), f32),
            pltpu.VMEM((slabs, near_x * tiles + 1, *tile), bf16),
            pltpu.VMEM((slabs, near_x * tiles + 1, *tile), bf16),
            pltpu.VMEM((slabs, near_x, tiles + 1, *tile), bf16),
            pltpu.VMEM((slabs, near_x - 1, tiles + 1, *tile), bf16),
            pltpu.VMEM((slabs, tiles, *tile), bf16),
            pltpu.VMEM((batches, replicas, *tile), bf16),
            pltpu.VMEM((batches, replicas, *tile), bf16),
            dma((3,)),
            *[dma((slabs,))] * 12,
            *[dma((batches,))] * 2,
        ],
        compiler_params=pltpu.CompilerParams(
            collective_id=0, has_side_effects=True, vmem_limit_bytes=56 << 20
        ),
        name="layer_sections",
    )(hidden_in, gains, weights.reshape(width, page))
    positions = jnp.arange(slots, dtype=jnp.int32)
    return jnp.where((positions < lengths[0])[:, None], states, jnp.zeros_like(states))[None]


def solution(mesh):
    sizes = tuple(mesh.shape[axis] for axis in ("replica", "section", "tp"))
    return jax.shard_map(
        functools.partial(local, sizes),
        mesh=mesh,
        in_specs=(
            P("replica", "tp"),
            P("section", "tp"),
            P("section", "tp", "replica", None),
            P("replica"),
        ),
        out_specs=P("section", "replica", "tp"),
        check_vma=False,
    )
```

```python
import functools

import jax
import jax.numpy as jnp
from jax import lax
from jax.experimental import pallas as pl
from jax.experimental.pallas import tpu as pltpu
from jax.sharding import PartitionSpec as P

EPSILON = 1e-06
MESH = pl.DeviceIdType.MESH
NEAR_Y = 4
CORES = 2
ROWS = 8
HIGH = 16
LANES = 128
HALF = LANES // 2
BATCH = 2 * HIGH // ROWS

STAGES = dict(along_z=0.0, along_y=4, product=9, pair=10.5, update=14)
PAGES, PLACE = 14.1, 60
INTERVAL = 3


def order_of(slabs):
    events = [(m * INTERVAL + offset, m, name) for m in range(slabs) for name, offset in STAGES.items()]
    for batch in range(slabs // BATCH):
        last = (batch + 1) * BATCH - 1
        events += [(last * INTERVAL + PAGES, batch, "pages"), (last * INTERVAL + PLACE, batch, "place")]
    return [(name, index) for _, index, name in sorted(events, key=lambda e: (e[0], e[1]))]


def kernel(
    sizes, hid_hbm, gain_hbm, w_hbm, out_ref,
    hid_ref, gain_ref, w_raw, w_ref, ones,
    gathered, rows_in, residual, squares, mine, core_out, core_in, x_out, x_in, new_out, page_out, page_in,
    in_sem, hop_s, hop_r, z_s, z_r, e_s, e_r, y_s, y_r, c_s, c_r, x_s, x_r, p_s, p_r,
):
    replicas, sections, groups, slabs = sizes
    near_y, near_z, near_x = NEAR_Y, replicas // NEAR_Y, groups // CORES
    row_groups = replicas * ROWS // HIGH
    tiles = row_groups // 2
    width, page = w_raw.shape
    column_tiles = width // LANES
    bf16, f32 = jnp.bfloat16, jnp.float32

    replica, section, tp = lax.axis_index("replica"), lax.axis_index("section"), lax.axis_index("tp")
    z, y = replica // near_y, replica % near_y
    x, core = tp // CORES, tp % CORES

    def place_of(z_to=z, y_to=y, x_to=x, core_to=core, section_to=section):
        return (z_to * near_y + y_to, section_to, x_to * CORES + core_to)

    def send(src, dst, send_sem, recv_sem, device):
        pltpu.make_async_remote_copy(
            src_ref=src, dst_ref=dst, send_sem=send_sem, recv_sem=recv_sem, device_id=device, device_id_type=MESH
        ).start()

    def wait(ref, sem):
        pltpu.make_async_copy(ref, ref, sem).wait()

    lane = lax.broadcasted_iota(jnp.int32, (HIGH, LANES), 1)
    low = lane < HALF
    high_part = lane % 8 < 4

    def turn(value):
        return pltpu.roll(value, HALF, 1)

    def lows(left, right):
        return jnp.where(low, left, turn(right))

    def highs(left, right):
        return jnp.where(low, turn(left), right)

    def two_parts(value):
        high = value.astype(bf16).astype(f32)
        return jnp.where(high_part, high, value - high)

    def one_value(parts):
        return parts + jnp.where(high_part, pltpu.roll(parts, LANES - 4, 1), pltpu.roll(parts, 4, 1))

    def stack(above, below):
        return jnp.concatenate([above, below], axis=0)

    def slot_of(z_from):
        return (z_from - z + near_z) % near_z

    def load_hidden():
        return pltpu.make_async_copy(hid_hbm, hid_ref, in_sem.at[0])

    def load_gains():
        return pltpu.make_async_copy(gain_hbm, gain_ref, in_sem.at[1])

    def load_weights():
        return pltpu.make_async_copy(w_hbm, w_raw, in_sem.at[2])

    @pl.when(section == 0)
    def _():
        load_hidden().start()

    load_gains().start()
    load_weights().start()

    barrier = pltpu.get_barrier_semaphore()

    def greet(device):
        pl.semaphore_signal(barrier, inc=1, device_id=device, device_id_type=MESH)

    @pl.when(section > 0)
    def _():
        greet(place_of(section_to=section - 1))

    for dz in range(near_z):
        for dy in range(near_y):
            if dz or dy:
                greet(place_of((z + dz) % near_z, (y + dy) % near_y))
    greet(place_of(core_to=1 - core))
    for dx in range(1, near_x):
        greet(place_of(x_to=(x + dx) % near_x))

    @pl.when(section == 0)
    def _():
        load_hidden().wait()

        def of_pair(pair, _):
            rows = pl.ds(pl.multiple_of(pair * HIGH, HIGH), HIGH)
            for t in range(tiles):
                left = hid_ref[rows, pl.ds(t * LANES, LANES)].astype(f32)
                right = hid_ref[rows, pl.ds((t + tiles) * LANES, LANES)].astype(f32)
                gathered[2 * pair, y, 0, t] = stack(left[:ROWS], right[:ROWS]).astype(bf16)
                gathered[2 * pair + 1, y, 0, t] = stack(left[ROWS:], right[ROWS:]).astype(bf16)
            return 0

        lax.fori_loop(0, slabs // 2, of_pair, 0)

    pl.semaphore_wait(barrier, replicas + near_x - 1 + jnp.where(section < sections - 1, 1, 0))

    def along_z(m):
        block = gathered.at[m, y, 0]

        @pl.when(section > 0)
        def _():
            wait(block, hop_r.at[m])

        for dz in range(1, near_z):
            send(block, gathered.at[m, y, near_z - dz], z_s.at[m], z_r.at[m], place_of(z_to=(z + dz) % near_z))
        for dy in range(1, near_y):
            send(block, block, e_s.at[m], e_r.at[m], place_of(y_to=(y + dy) % near_y))

    def along_y(m):
        block = gathered.at[m, y, pl.ds(1, near_z - 1)]
        wait(block, z_r.at[m])
        for dy in range(1, near_y):
            send(block, block, y_s.at[m], y_r.at[m], place_of(y_to=(y + dy) % near_y))

    def prepare():
        load_gains().wait()
        load_weights().wait()
        ones[...] = jnp.ones_like(ones)
        wide_low = lax.broadcasted_iota(jnp.int32, (LANES, LANES), 1) < HALF

        def of_rows(k, _):
            rows = pl.ds(pl.multiple_of(k * LANES, LANES), LANES)
            gain = jnp.transpose(jnp.broadcast_to(gain_ref[:, rows], (LANES, LANES)))
            for j in range(near_x // 2):
                left = w_raw[rows, pl.ds(2 * j * LANES, LANES)].astype(f32) * gain
                right = w_raw[rows, pl.ds((2 * j + 1) * LANES, LANES)].astype(f32) * gain
                of_0 = jnp.where(wide_low, left, turn(right))
                of_1 = jnp.where(wide_low, turn(left), right)
                w_ref[rows, pl.ds(j * LANES, LANES)] = of_0.astype(bf16)
                w_ref[rows, pl.ds((near_x // 2 + j) * LANES, LANES)] = of_1.astype(bf16)
            return 0

        lax.fori_loop(0, column_tiles, of_rows, 0)

    def product(m):
        wait(gathered.at[m, pl.ds(0, near_y - 1), 0], e_r.at[m])
        wait(gathered.at[m, pl.ds(0, near_y - 1), pl.ds(1, near_z - 1)], y_r.at[m])
        slots = [slot_of(z_from) for z_from in range(near_z)]

        @pl.when(section == 0)
        def _():
            def chunks(group):
                y_from, z_from = 2 * group // near_z, 2 * group % near_z
                return y_from, slots[z_from], slots[z_from + 1]

            for group in range(row_groups):
                y_from, first, second = chunks(group)
                rows = pl.ds(group * HIGH, HIGH)
                for t in range(tiles):
                    one = gathered[m, y_from, first, t].astype(f32)
                    two = gathered[m, y_from, second, t].astype(f32)
                    rows_in[rows, pl.ds(t * LANES, LANES)] = stack(one[:ROWS], two[:ROWS]).astype(bf16)
                    rows_in[rows, pl.ds((t + tiles) * LANES, LANES)] = stack(one[ROWS:], two[ROWS:]).astype(bf16)

            odd = replica % 2 == 1
            column = replica // 2
            upper = column >= tiles

            def own_columns(group):
                y_from, first, second = chunks(group)
                one = gathered[m, y_from, first, column % tiles].astype(f32)
                two = gathered[m, y_from, second, column % tiles].astype(f32)
                return jnp.where(upper, stack(one[ROWS:], two[ROWS:]), stack(one[:ROWS], two[:ROWS]))

            for a in range(tiles):
                left, right = own_columns(a), own_columns(a + tiles)
                residual[m, a] = jnp.where(odd, highs(left, right), lows(left, right)).astype(bf16)

        @pl.when(section > 0)
        def _():
            for a in range(tiles):
                top, bottom = pl.ds(a * HIGH, HIGH), pl.ds((a + tiles) * HIGH, HIGH)
                for k in range(column_tiles):
                    columns = pl.ds(k * LANES, LANES)
                    y_from, slot = 2 * k % near_y, slots[2 * k // near_y]
                    left = gathered[m, y_from, slot, a]
                    right = gathered[m, y_from + 1, slot, a]
                    rows_in[top, columns] = jnp.concatenate([left[:, :HALF], right[:, :HALF]], axis=1)
                    rows_in[bottom, columns] = jnp.concatenate([left[:, HALF:], right[:, HALF:]], axis=1)

            residual[m] = gathered[m, y, 0]

        value = rows_in[...]
        all_squares = jnp.dot(value * value, ones[...], preferred_element_type=f32)
        parts = jnp.zeros((HIGH, LANES), f32)
        for group in range(row_groups):
            parts = jnp.where(lane // 8 == group, all_squares[group * HIGH : (group + 1) * HIGH], parts)
        squares[m] = two_parts(parts)
        core_out[m, row_groups * near_x // 2] = squares[m].astype(bf16)
        theirs = pl.ds(pl.multiple_of((1 - core) * (page // 2), page // 2), page // 2)
        result = jnp.dot(value, w_ref[:, theirs], preferred_element_type=f32).astype(bf16)
        for k in range(near_x // 2):
            core_out[m, pl.ds(k * row_groups, row_groups)] = result[:, k * LANES : (k + 1) * LANES].reshape(
                row_groups, HIGH, LANES
            )
        send(core_out.at[m], core_in.at[m], c_s.at[m], c_r.at[m], place_of(core_to=1 - core))
        own = pl.ds(pl.multiple_of(core * (page // 2), page // 2), page // 2)
        mine[m] = jnp.dot(value, w_ref[:, own], preferred_element_type=f32)

    def pair(m):
        wait(core_in.at[m], c_r.at[m])
        parts = squares[m] + core_in[m, row_groups * near_x // 2].astype(f32)
        parts = two_parts(one_value(parts)).astype(bf16)
        for k in range(near_x // 2):
            def total(group):
                rows, columns = pl.ds(group * HIGH, HIGH), pl.ds(k * LANES, LANES)
                return mine[m, rows, columns] + core_in[m, k * row_groups + group].astype(f32)

            for a in range(tiles):
                left, right = total(a), total(a + tiles)
                x_out[m, 2 * k, a] = lows(left, right).astype(bf16)
                x_out[m, 2 * k + 1, a] = highs(left, right).astype(bf16)
        for j in range(near_x):
            x_out[m, j, tiles] = parts
        for dx in range(1, near_x):
            to = (x + dx) % near_x
            send(x_out.at[m, to], x_in.at[m, dx - 1], x_s.at[m], x_r.at[m], place_of(x_to=to))

    def update(m):
        wait(x_in.at[m], x_r.at[m])

        def total(a):
            value = x_out[m, x, a].astype(f32)
            for dx in range(1, near_x):
                value += x_in[m, dx - 1, a].astype(f32)
            return value

        inverse = lax.rsqrt(one_value(total(tiles)) / (width * groups) + EPSILON)
        for a in range(tiles):
            b = a + tiles
            factor = jnp.where(low, inverse[:, 8 * a : 8 * a + 1], inverse[:, 8 * b : 8 * b + 1])
            new_out[m, a] = (residual[m, a].astype(f32) + factor * total(a)).astype(bf16)

        @pl.when(section < sections - 1)
        def _():
            send(new_out.at[m], gathered.at[m, y, 0], hop_s.at[m], hop_r.at[m], place_of(section_to=section + 1))

    def pages(batch):
        for q in range(replicas):
            group, part = q * ROWS // HIGH, q * ROWS % HIGH
            piece = [
                new_out[batch * BATCH + i, group % tiles].astype(f32)[part : part + ROWS] for i in range(BATCH)
            ]
            left, right = stack(piece[0], piece[1]), stack(piece[2], piece[3])
            page_out[batch, q] = (lows if group < tiles else highs)(left, right).astype(bf16)
            y_to, z_to = q // near_z, q % near_z
            src, dst = page_out.at[batch, q], page_in.at[batch, replica]
            here = (z_to == z) & (y_to == y)

            @pl.when(here)
            def _(src=src, dst=dst):
                pltpu.make_async_copy(src, dst, p_r.at[batch]).start()

            @pl.when(jnp.logical_not(here))
            def _(src=src, dst=dst, z_to=z_to, y_to=y_to):
                send(src, dst, p_s.at[batch], p_r.at[batch], place_of(z_to, y_to))

    def place(batch):
        wait(page_in.at[batch], p_r.at[batch])
        row = batch * BATCH * ROWS
        for k in range(column_tiles):
            columns = pl.ds(k * LANES, LANES)
            left, right = page_in[batch, 2 * k].astype(f32), page_in[batch, 2 * k + 1].astype(f32)
            out_ref[pl.ds(row, HIGH), columns] = lows(left, right).astype(bf16)
            out_ref[pl.ds(row + HIGH, HIGH), columns] = highs(left, right).astype(bf16)

    stages = dict(
        along_z=along_z, along_y=along_y, product=product, pair=pair, update=update, pages=pages, place=place
    )
    loaded = False
    for name, index in order_of(slabs):
        if name == "product" and not loaded:
            prepare()
            loaded = True
        stages[name](index)

    for m in range(slabs):
        wait(gathered.at[m, 0, pl.ds(1, near_z - 1)], z_s.at[m])
        wait(gathered.at[m, pl.ds(0, near_y - 1), 0], e_s.at[m])
        wait(gathered.at[m, pl.ds(0, near_y - 1), pl.ds(1, near_z - 1)], y_s.at[m])
        wait(core_out.at[m], c_s.at[m])
        wait(x_in.at[m], x_s.at[m])

        @pl.when(section < sections - 1)
        def _(m=m):
            wait(new_out.at[m], hop_s.at[m])

    for batch in range(slabs // BATCH):
        wait(page_in.at[batch, pl.ds(0, replicas - 1)], p_s.at[batch])


def local(sizes, hidden_in, gains, weights, lengths):
    replicas, sections, groups = sizes
    slots, width = hidden_in.shape
    page = weights.shape[3]
    slabs = slots // ROWS
    batches = slabs // BATCH
    near_z, near_x = replicas // NEAR_Y, groups // CORES
    rows = replicas * ROWS
    tiles = rows // HIGH // 2
    bf16, f32 = jnp.bfloat16, jnp.float32
    tile = (HIGH, LANES)
    dma = pltpu.SemaphoreType.DMA
    states = pl.pallas_call(
        functools.partial(kernel, (*sizes, slabs)),
        out_shape=jax.ShapeDtypeStruct((slots, width), bf16),
        in_specs=[pl.BlockSpec(memory_space=pl.ANY)] * 3,
        out_specs=pl.BlockSpec(memory_space=pltpu.VMEM),
        scratch_shapes=[
            pltpu.VMEM((slots, width), bf16),
            pltpu.VMEM((1, width), f32),
            pltpu.VMEM((width, page), bf16),
            pltpu.VMEM((width, page), bf16),
            pltpu.VMEM((width, LANES), bf16),
            pltpu.VMEM((slabs, NEAR_Y, near_z, tiles, *tile), bf16),
            pltpu.VMEM((rows, width), bf16),
            pltpu.VMEM((slabs, tiles, *tile), bf16),
            pltpu.VMEM((slabs, *tile), f32),
            pltpu.VMEM((slabs, rows, page // 2), f32),
            pltpu.VMEM((slabs, near_x * tiles + 1, *tile), bf16),
            pltpu.VMEM((slabs, near_x * tiles + 1, *tile), bf16),
            pltpu.VMEM((slabs, near_x, tiles + 1, *tile), bf16),
            pltpu.VMEM((slabs, near_x - 1, tiles + 1, *tile), bf16),
            pltpu.VMEM((slabs, tiles, *tile), bf16),
            pltpu.VMEM((batches, replicas, *tile), bf16),
            pltpu.VMEM((batches, replicas, *tile), bf16),
            dma((3,)),
            *[dma((slabs,))] * 12,
            *[dma((batches,))] * 2,
        ],
        compiler_params=pltpu.CompilerParams(
            collective_id=0, has_side_effects=True, vmem_limit_bytes=56 << 20
        ),
        name="layer_sections",
    )(hidden_in, gains, weights.reshape(width, page))
    positions = jnp.arange(slots, dtype=jnp.int32)
    return jnp.where((positions < lengths[0])[:, None], states, jnp.zeros_like(states))[None]


def solution(mesh):
    sizes = tuple(mesh.shape[axis] for axis in ("replica", "section", "tp"))
    return jax.shard_map(
        functools.partial(local, sizes),
        mesh=mesh,
        in_specs=(
            P("replica", "tp"),
            P("section", "tp"),
            P("section", "tp", "replica", None),
            P("replica"),
        ),
        out_specs=P("section", "replica", "tp"),
        check_vma=False,
    )
```

```python
import functools

import jax
import jax.numpy as jnp
from jax import lax
from jax.experimental import pallas as pl
from jax.experimental.pallas import tpu as pltpu
from jax.sharding import PartitionSpec as P

EPSILON = 1e-06
MESH = pl.DeviceIdType.MESH
NEAR_Y = 4
CORES = 2
ROWS = 8
HIGH = 16
LANES = 128
HALF = LANES // 2
BATCH = 2 * HIGH // ROWS

STAGES = dict(along_z=0.0, along_y=4, product=9, pair=10.5, update=14)
PAGES, PLACE = 14.1, 60
INTERVAL = 3


def order_of(slabs):
    events = [(m * INTERVAL + offset, m, name) for m in range(slabs) for name, offset in STAGES.items()]
    for batch in range(slabs // BATCH):
        last = (batch + 1) * BATCH - 1
        events += [(last * INTERVAL + PAGES, batch, "pages"), (last * INTERVAL + PLACE, batch, "place")]
    return [(name, index) for _, index, name in sorted(events, key=lambda e: (e[0], e[1]))]


def kernel(
    sizes, hid_hbm, gain_hbm, w_hbm, out_ref,
    hid_ref, gain_ref, w_raw, w_ref, ones,
    gathered, rows_in, residual, squares, mine, core_out, core_in, x_out, x_in, new_out, page_out, page_in,
    in_sem, hop_s, hop_r, z_s, z_r, e_s, e_r, y_s, y_r, c_s, c_r, x_s, x_r, p_s, p_r,
):
    replicas, sections, groups, slabs = sizes
    near_y, near_z, near_x = NEAR_Y, replicas // NEAR_Y, groups // CORES
    row_groups = replicas * ROWS // HIGH
    tiles = row_groups // 2
    width, page = w_raw.shape
    column_tiles = width // LANES
    bf16, f32 = jnp.bfloat16, jnp.float32

    replica, section, tp = lax.axis_index("replica"), lax.axis_index("section"), lax.axis_index("tp")
    z, y = replica // near_y, replica % near_y
    x, core = tp // CORES, tp % CORES

    def place_of(z_to=z, y_to=y, x_to=x, core_to=core, section_to=section):
        return (z_to * near_y + y_to, section_to, x_to * CORES + core_to)

    def send(src, dst, send_sem, recv_sem, device):
        pltpu.make_async_remote_copy(
            src_ref=src, dst_ref=dst, send_sem=send_sem, recv_sem=recv_sem, device_id=device, device_id_type=MESH
        ).start()

    def wait(ref, sem):
        pltpu.make_async_copy(ref, ref, sem).wait()

    lane = lax.broadcasted_iota(jnp.int32, (HIGH, LANES), 1)
    low = lane < HALF
    high_part = lane % 8 < 4

    def turn(value):
        return pltpu.roll(value, HALF, 1)

    def lows(left, right):
        return jnp.where(low, left, turn(right))

    def highs(left, right):
        return jnp.where(low, turn(left), right)

    def two_parts(value):
        high = value.astype(bf16).astype(f32)
        return jnp.where(high_part, high, value - high)

    def one_value(parts):
        return parts + jnp.where(high_part, pltpu.roll(parts, LANES - 4, 1), pltpu.roll(parts, 4, 1))

    def stack(above, below):
        return jnp.concatenate([above, below], axis=0)

    def slot_of(z_from):
        return (z_from - z + near_z) % near_z

    def load_hidden():
        return pltpu.make_async_copy(hid_hbm, hid_ref, in_sem.at[0])

    def load_gains():
        return pltpu.make_async_copy(gain_hbm, gain_ref, in_sem.at[1])

    def load_weights():
        return pltpu.make_async_copy(w_hbm, w_raw, in_sem.at[2])

    @pl.when(section == 0)
    def _():
        load_hidden().start()

    load_gains().start()
    load_weights().start()

    barrier = pltpu.get_barrier_semaphore()

    def greet(device):
        pl.semaphore_signal(barrier, inc=1, device_id=device, device_id_type=MESH)

    @pl.when(section > 0)
    def _():
        greet(place_of(section_to=section - 1))

    for dz in range(near_z):
        for dy in range(near_y):
            if dz or dy:
                greet(place_of((z + dz) % near_z, (y + dy) % near_y))
    greet(place_of(core_to=1 - core))
    for dx in range(1, near_x):
        greet(place_of(x_to=(x + dx) % near_x))

    @pl.when(section == 0)
    def _():
        load_hidden().wait()

        def of_pair(pair, _):
            rows = pl.ds(pl.multiple_of(pair * HIGH, HIGH), HIGH)
            for t in range(tiles):
                left = hid_ref[rows, pl.ds(t * LANES, LANES)].astype(f32)
                right = hid_ref[rows, pl.ds((t + tiles) * LANES, LANES)].astype(f32)
                gathered[2 * pair, y, 0, t] = stack(left[:ROWS], right[:ROWS]).astype(bf16)
                gathered[2 * pair + 1, y, 0, t] = stack(left[ROWS:], right[ROWS:]).astype(bf16)
            return 0

        lax.fori_loop(0, slabs // 2, of_pair, 0)

    pl.semaphore_wait(barrier, replicas + near_x - 1 + jnp.where(section < sections - 1, 1, 0))

    def along_z(m):
        block = gathered.at[m, y, 0]

        @pl.when(section > 0)
        def _():
            wait(block, hop_r.at[m])

        for dz in range(1, near_z):
            send(block, gathered.at[m, y, near_z - dz], z_s.at[m], z_r.at[m], place_of(z_to=(z + dz) % near_z))
        for dy in (2, 1, near_y - 1):
            send(block, block, e_s.at[m], e_r.at[m], place_of(y_to=(y + dy) % near_y))

    def along_y(m):
        block = gathered.at[m, y, pl.ds(1, near_z - 1)]
        wait(block, z_r.at[m])
        for dy in (2, 1, near_y - 1):
            send(block, block, y_s.at[m], y_r.at[m], place_of(y_to=(y + dy) % near_y))

    def prepare():
        load_gains().wait()
        load_weights().wait()
        ones[...] = jnp.ones_like(ones)
        wide_low = lax.broadcasted_iota(jnp.int32, (LANES, LANES), 1) < HALF

        def of_rows(k, _):
            rows = pl.ds(pl.multiple_of(k * LANES, LANES), LANES)
            gain = jnp.transpose(jnp.broadcast_to(gain_ref[:, rows], (LANES, LANES)))
            for j in range(near_x // 2):
                left = w_raw[rows, pl.ds(2 * j * LANES, LANES)].astype(f32) * gain
                right = w_raw[rows, pl.ds((2 * j + 1) * LANES, LANES)].astype(f32) * gain
                of_0 = jnp.where(wide_low, left, turn(right))
                of_1 = jnp.where(wide_low, turn(left), right)
                w_ref[rows, pl.ds(j * LANES, LANES)] = of_0.astype(bf16)
                w_ref[rows, pl.ds((near_x // 2 + j) * LANES, LANES)] = of_1.astype(bf16)
            return 0

        lax.fori_loop(0, column_tiles, of_rows, 0)

    def product(m):
        wait(gathered.at[m, pl.ds(0, near_y - 1), 0], e_r.at[m])
        wait(gathered.at[m, pl.ds(0, near_y - 1), pl.ds(1, near_z - 1)], y_r.at[m])
        slots = [slot_of(z_from) for z_from in range(near_z)]

        @pl.when(section == 0)
        def _():
            def chunks(group):
                y_from, z_from = 2 * group // near_z, 2 * group % near_z
                return y_from, slots[z_from], slots[z_from + 1]

            for group in range(row_groups):
                y_from, first, second = chunks(group)
                rows = pl.ds(group * HIGH, HIGH)
                for t in range(tiles):
                    one = gathered[m, y_from, first, t].astype(f32)
                    two = gathered[m, y_from, second, t].astype(f32)
                    rows_in[rows, pl.ds(t * LANES, LANES)] = stack(one[:ROWS], two[:ROWS]).astype(bf16)
                    rows_in[rows, pl.ds((t + tiles) * LANES, LANES)] = stack(one[ROWS:], two[ROWS:]).astype(bf16)

            odd = replica % 2 == 1
            column = replica // 2
            upper = column >= tiles

            def own_columns(group):
                y_from, first, second = chunks(group)
                one = gathered[m, y_from, first, column % tiles].astype(f32)
                two = gathered[m, y_from, second, column % tiles].astype(f32)
                return jnp.where(upper, stack(one[ROWS:], two[ROWS:]), stack(one[:ROWS], two[:ROWS]))

            for a in range(tiles):
                left, right = own_columns(a), own_columns(a + tiles)
                residual[m, a] = jnp.where(odd, highs(left, right), lows(left, right)).astype(bf16)

        @pl.when(section > 0)
        def _():
            for a in range(tiles):
                top, bottom = pl.ds(a * HIGH, HIGH), pl.ds((a + tiles) * HIGH, HIGH)
                for k in range(column_tiles):
                    columns = pl.ds(k * LANES, LANES)
                    y_from, slot = 2 * k % near_y, slots[2 * k // near_y]
                    left = gathered[m, y_from, slot, a]
                    right = gathered[m, y_from + 1, slot, a]
                    rows_in[top, columns] = jnp.concatenate([left[:, :HALF], right[:, :HALF]], axis=1)
                    rows_in[bottom, columns] = jnp.concatenate([left[:, HALF:], right[:, HALF:]], axis=1)

            residual[m] = gathered[m, y, 0]

        value = rows_in[...]
        all_squares = jnp.dot(value * value, ones[...], preferred_element_type=f32)
        parts = jnp.zeros((HIGH, LANES), f32)
        for group in range(row_groups):
            parts = jnp.where(lane // 8 == group, all_squares[group * HIGH : (group + 1) * HIGH], parts)
        squares[m] = two_parts(parts)
        core_out[m, row_groups * near_x // 2] = squares[m].astype(bf16)
        theirs = pl.ds(pl.multiple_of((1 - core) * (page // 2), page // 2), page // 2)
        result = jnp.dot(value, w_ref[:, theirs], preferred_element_type=f32).astype(bf16)
        for k in range(near_x // 2):
            core_out[m, pl.ds(k * row_groups, row_groups)] = result[:, k * LANES : (k + 1) * LANES].reshape(
                row_groups, HIGH, LANES
            )
        send(core_out.at[m], core_in.at[m], c_s.at[m], c_r.at[m], place_of(core_to=1 - core))
        own = pl.ds(pl.multiple_of(core * (page // 2), page // 2), page // 2)
        mine[m] = jnp.dot(value, w_ref[:, own], preferred_element_type=f32)

    def pair(m):
        wait(core_in.at[m], c_r.at[m])
        parts = squares[m] + core_in[m, row_groups * near_x // 2].astype(f32)
        parts = two_parts(one_value(parts)).astype(bf16)
        for k in range(near_x // 2):
            def total(group):
                rows, columns = pl.ds(group * HIGH, HIGH), pl.ds(k * LANES, LANES)
                return mine[m, rows, columns] + core_in[m, k * row_groups + group].astype(f32)

            for a in range(tiles):
                left, right = total(a), total(a + tiles)
                x_out[m, 2 * k, a] = lows(left, right).astype(bf16)
                x_out[m, 2 * k + 1, a] = highs(left, right).astype(bf16)
        for j in range(near_x):
            x_out[m, j, tiles] = parts
        for dx in range(1, near_x):
            to = (x + dx) % near_x
            send(x_out.at[m, to], x_in.at[m, dx - 1], x_s.at[m], x_r.at[m], place_of(x_to=to))

    def update(m):
        wait(x_in.at[m], x_r.at[m])

        def total(a):
            value = x_out[m, x, a].astype(f32)
            for dx in range(1, near_x):
                value += x_in[m, dx - 1, a].astype(f32)
            return value

        inverse = lax.rsqrt(one_value(total(tiles)) / (width * groups) + EPSILON)
        for a in range(tiles):
            b = a + tiles
            factor = jnp.where(low, inverse[:, 8 * a : 8 * a + 1], inverse[:, 8 * b : 8 * b + 1])
            new_out[m, a] = (residual[m, a].astype(f32) + factor * total(a)).astype(bf16)

        @pl.when(section < sections - 1)
        def _():
            send(new_out.at[m], gathered.at[m, y, 0], hop_s.at[m], hop_r.at[m], place_of(section_to=section + 1))

    def pages(batch):
        for q in range(replicas):
            group, part = q * ROWS // HIGH, q * ROWS % HIGH
            piece = [
                new_out[batch * BATCH + i, group % tiles].astype(f32)[part : part + ROWS] for i in range(BATCH)
            ]
            left, right = stack(piece[0], piece[1]), stack(piece[2], piece[3])
            page_out[batch, q] = (lows if group < tiles else highs)(left, right).astype(bf16)
            y_to, z_to = q // near_z, q % near_z
            src, dst = page_out.at[batch, q], page_in.at[batch, replica]
            here = (z_to == z) & (y_to == y)

            @pl.when(here)
            def _(src=src, dst=dst):
                pltpu.make_async_copy(src, dst, p_r.at[batch]).start()

            @pl.when(jnp.logical_not(here))
            def _(src=src, dst=dst, z_to=z_to, y_to=y_to):
                send(src, dst, p_s.at[batch], p_r.at[batch], place_of(z_to, y_to))

    def place(batch):
        wait(page_in.at[batch], p_r.at[batch])
        row = batch * BATCH * ROWS
        for k in range(column_tiles):
            columns = pl.ds(k * LANES, LANES)
            left, right = page_in[batch, 2 * k].astype(f32), page_in[batch, 2 * k + 1].astype(f32)
            out_ref[pl.ds(row, HIGH), columns] = lows(left, right).astype(bf16)
            out_ref[pl.ds(row + HIGH, HIGH), columns] = highs(left, right).astype(bf16)

    stages = dict(
        along_z=along_z, along_y=along_y, product=product, pair=pair, update=update, pages=pages, place=place
    )
    def sent(m):
        wait(gathered.at[m, 0, pl.ds(1, near_z - 1)], z_s.at[m])
        wait(gathered.at[m, pl.ds(0, near_y - 1), 0], e_s.at[m])
        wait(gathered.at[m, pl.ds(0, near_y - 1), pl.ds(1, near_z - 1)], y_s.at[m])
        wait(core_out.at[m], c_s.at[m])
        wait(x_in.at[m], x_s.at[m])

        @pl.when(section < sections - 1)
        def _():
            wait(new_out.at[m], hop_s.at[m])

    loaded = False
    order = order_of(slabs)
    for step, (name, index) in enumerate(order):
        if name == "product" and not loaded:
            prepare()
            loaded = True
        if step == len(order) - 1:
            for m in range(slabs):
                sent(m)
        stages[name](index)

    for batch in range(slabs // BATCH):
        wait(page_in.at[batch, pl.ds(0, replicas - 1)], p_s.at[batch])


def local(sizes, hidden_in, gains, weights, lengths):
    replicas, sections, groups = sizes
    slots, width = hidden_in.shape
    page = weights.shape[3]
    slabs = slots // ROWS
    batches = slabs // BATCH
    near_z, near_x = replicas // NEAR_Y, groups // CORES
    rows = replicas * ROWS
    tiles = rows // HIGH // 2
    bf16, f32 = jnp.bfloat16, jnp.float32
    tile = (HIGH, LANES)
    dma = pltpu.SemaphoreType.DMA
    states = pl.pallas_call(
        functools.partial(kernel, (*sizes, slabs)),
        out_shape=jax.ShapeDtypeStruct((slots, width), bf16),
        in_specs=[pl.BlockSpec(memory_space=pl.ANY)] * 3,
        out_specs=pl.BlockSpec(memory_space=pltpu.VMEM),
        scratch_shapes=[
            pltpu.VMEM((slots, width), bf16),
            pltpu.VMEM((1, width), f32),
            pltpu.VMEM((width, page), bf16),
            pltpu.VMEM((width, page), bf16),
            pltpu.VMEM((width, LANES), bf16),
            pltpu.VMEM((slabs, NEAR_Y, near_z, tiles, *tile), bf16),
            pltpu.VMEM((rows, width), bf16),
            pltpu.VMEM((slabs, tiles, *tile), bf16),
            pltpu.VMEM((slabs, *tile), f32),
            pltpu.VMEM((slabs, rows, page // 2), f32),
            pltpu.VMEM((slabs, near_x * tiles + 1, *tile), bf16),
            pltpu.VMEM((slabs, near_x * tiles + 1, *tile), bf16),
            pltpu.VMEM((slabs, near_x, tiles + 1, *tile), bf16),
            pltpu.VMEM((slabs, near_x - 1, tiles + 1, *tile), bf16),
            pltpu.VMEM((slabs, tiles, *tile), bf16),
            pltpu.VMEM((batches, replicas, *tile), bf16),
            pltpu.VMEM((batches, replicas, *tile), bf16),
            dma((3,)),
            *[dma((slabs,))] * 12,
            *[dma((batches,))] * 2,
        ],
        compiler_params=pltpu.CompilerParams(
            collective_id=0, has_side_effects=True, vmem_limit_bytes=56 << 20
        ),
        name="layer_sections",
    )(hidden_in, gains, weights.reshape(width, page))
    positions = jnp.arange(slots, dtype=jnp.int32)
    return jnp.where((positions < lengths[0])[:, None], states, jnp.zeros_like(states))[None]


def solution(mesh):
    sizes = tuple(mesh.shape[axis] for axis in ("replica", "section", "tp"))
    return jax.shard_map(
        functools.partial(local, sizes),
        mesh=mesh,
        in_specs=(
            P("replica", "tp"),
            P("section", "tp"),
            P("section", "tp", "replica", None),
            P("replica"),
        ),
        out_specs=P("section", "replica", "tp"),
        check_vma=False,
    )
```
